32 devices in a mesh: dp: 8 (over z, x), tensor: 4 (over y, core).
Axes of the slice: x: 2, y: 2, z: 4, core: 2. Of those that a mesh axis runs over, the one named last changes fastest.
Arguments:
- tokens: bfloat16 [16384, 768], P(('dp', 'tensor')), may hold values from -6 to 6
- segment_ids: int32 [16, 1024], P('dp'), may hold values from 0 to 3, never falling along the last dimension, each value on 1 to 512 neighbouring positions
- ln1_gain: float32 [768], replicated, may hold values from 0.5 to 1.5
- ln1_bias: float32 [768], replicated, may hold values from -3 to 3
- w_qkv: bfloat16 [768, 3, 768], P(None, None, 'tensor'), may hold values from -0.21875 to 0.21875
- b_qv: float32 [2, 768], P(None, 'tensor'), may hold values from -3 to 3
- w_out: bfloat16 [768, 768], P('tensor'), may hold values from -0.875 to 0.875
- b_out: float32 [768], replicated, may hold values from -3 to 3
- ln2_gain: float32 [768], replicated, may hold values from 0.5 to 1.5
- ln2_bias: float32 [768], replicated, may hold values from -3 to 3
- w_fc: bfloat16 [768, 3072], P(None, 'tensor'), may hold values from -0.21875 to 0.21875
- b_fc: float32 [3072], P('tensor'), may hold values from -3 to 3
- w_proj: bfloat16 [3072, 768], P('tensor'), may hold values from -0.109375 to 0.109375
- b_proj: float32 [768], replicated, may hold values from -3 to 3
- cotangent: bfloat16 [16384, 768], P(('dp', 'tensor')), may hold values from -6 to 6
Outputs:
- output: bfloat16 [16384, 768], P(('dp', 'tensor'))
- d_tokens: float32 [16384, 768], P(('dp', 'tensor'))
- d_ln1_gain: float32 [768], replicated
- d_ln1_bias: float32 [768], replicated
- d_w_qkv: float32 [768, 3, 768], P(None, None, 'tensor')
- d_b_qv: float32 [2, 768], P(None, 'tensor')
- d_w_out: float32 [768, 768], P('tensor')
- d_b_out: float32 [768], replicated
- d_ln2_gain: float32 [768], replicated
- d_ln2_bias: float32 [768], replicated
- d_w_fc: float32 [768, 3072], P(None, 'tensor')
- d_b_fc: float32 [3072], P('tensor')
- d_w_proj: float32 [3072, 768], P('tensor')
- d_b_proj: float32 [768], replicated
The draws below stay inside these ranges and needn't reach their ends.
Inputs may be any that keep to these rules, and one draw needn't show every extreme that they name: `segment_ids`: within each packed sequence the document numbers never fall; every document holds 1 to 512 tokens, one exactly 512.
All inputs are finite; a program needn't handle non-finite values.
Results may differ from the reference program's by a relative error of at most 0.012.
Values may be sent and summed in bfloat16 or wider, within the bound.
A program may use at most 128 MiB of HBM per device.

```python
import math
import jax
import jax.numpy as jnp
import numpy as np
from jax import lax

D = 768
H = 12
HD = 64
FF = 3072
LEN = 1024
PACKS = 2
NPACKS = 16
TOKENS = 16384
N_DP = 8


def levels(rng, shape, shards, smallest, top_value):
    factor_of, own = 1.0, jax.random.fold_in(rng, 6)
    for dim, blocks in shards:
        steps = jnp.exp(jax.random.uniform(jax.random.fold_in(own, dim), (blocks,), jnp.float32, smallest / len(shards), top_value / len(shards)))
        factor_of = factor_of * jnp.repeat(steps, shape[dim] // blocks).reshape([-1 if axis == dim else 1 for axis in range(len(shape))])
    return factor_of


def split_up(number_of, total, limit, slope):
    weights = [(1 << 20) // math.isqrt(grade ** slope) + 1 for grade in range(2, number_of + 1)]
    rest, counts = total - limit - (number_of - 1), [1] * (number_of - 1)
    while rest > 0:
        movable = [i for i in range(number_of - 1) if counts[i] < limit]
        mass, remaining = sum([weights[i] for i in movable]), rest
        for i in movable:
            more = min(limit - counts[i], max(1, remaining * weights[i] // mass), rest)
            counts[i] = counts[i] + more
            rest = rest - more
    return np.array([limit] + counts)


def uneven_parts(rng, number_of, total, limit, slope):
    if number_of == 2:
        one = jax.random.randint(rng, (), max(1, total - limit), min(limit, total - 1) + 1)
        return jnp.stack([one, total - one])
    lengths = jnp.asarray(split_up(number_of, total, limit, slope), jnp.int32)
    pairs = (number_of - 1) // 2
    source_of, sink = lengths[1:1 + 2 * pairs:2], lengths[2:2 + 2 * pairs:2]
    room = jnp.minimum(source_of - 1, limit - sink)
    moved = jax.random.randint(jax.random.fold_in(rng, 1), (pairs,), 0, 1 << 20) % (room + 1)
    lengths = lengths.at[1:1 + 2 * pairs:2].set(source_of - moved).at[2:2 + 2 * pairs:2].set(sink + moved)
    return lengths[jax.random.permutation(jax.random.fold_in(rng, 2), number_of)]


def bell_draw(own_key, shape, width, most, cuts=(), held_as=jnp.bfloat16):
    level = levels(own_key, shape, cuts, -0.22, 0.18) if cuts else 1.0
    entries = jax.random.normal(own_key, shape, jnp.float32) * width * level
    return jnp.minimum(jnp.maximum(entries, -most), most).astype(held_as)


def setup_inputs(seed: int = 0) -> dict:
    key_of = jax.random.split(jax.random.key(seed), 16)
    tokens = bell_draw(key_of[0], (TOKENS, D), 1.0, 6.0, ((0, 32),))
    segment_ids = jax.vmap(lambda own: jnp.searchsorted(jnp.cumsum(uneven_parts(own, 4, LEN, LEN // 2, 0)), jnp.arange(LEN), side="right"))(jax.random.split(key_of[1], NPACKS)).reshape((NPACKS, LEN)).astype(jnp.int32)
    ln1_gain = jnp.clip(1.0 + 0.1 * jax.random.normal(key_of[2], (D,), jnp.float32), 0.5, 1.5)
    ln1_bias = bell_draw(key_of[3], (D,), 0.5, 3.0, (), jnp.float32)
    w_qkv = bell_draw(key_of[4], (D, 3, D), D ** -0.5, 0.21875, ((2, 4),))
    b_qv = bell_draw(key_of[5], (2, D), 0.5, 3.0, ((1, 4),), jnp.float32)
    w_out = bell_draw(key_of[6], (D, D), (D // 16) ** -0.5, 0.875, ((0, 4),))
    b_out = bell_draw(key_of[7], (D,), 0.5, 3.0, (), jnp.float32)
    ln2_gain = jnp.clip(1.0 + 0.1 * jax.random.normal(key_of[8], (D,), jnp.float32), 0.5, 1.5)
    ln2_bias = bell_draw(key_of[9], (D,), 0.5, 3.0, (), jnp.float32)
    w_fc = bell_draw(key_of[10], (D, FF), D ** -0.5, 0.21875, ((1, 4),))
    b_fc = bell_draw(key_of[11], (FF,), 0.5, 3.0, ((0, 4),), jnp.float32)
    w_proj = bell_draw(key_of[12], (FF, D), FF ** -0.5, 0.109375, ((0, 4),))
    b_proj = bell_draw(key_of[13], (D,), 0.5, 3.0, (), jnp.float32)
    cotangent = bell_draw(key_of[14], (TOKENS, D), 1.0, 6.0, ((0, 32),))
    return {"tokens": tokens, "segment_ids": segment_ids, "ln1_gain": ln1_gain, "ln1_bias": ln1_bias, "w_qkv": w_qkv, "b_qv": b_qv, "w_out": w_out, "b_out": b_out, "ln2_gain": ln2_gain, "ln2_bias": ln2_bias, "w_fc": w_fc, "b_fc": b_fc, "w_proj": w_proj, "b_proj": b_proj, "cotangent": cotangent}


@jax.custom_vjp
def low(v):
    return lax.optimization_barrier(v.astype(jnp.bfloat16)).astype(jnp.float32)

@jax.custom_vjp
def low_back(v):
    return v

def low_keep(v):
    return (low(v), None)

def low_pass(kept, grad):
    return (grad,)

def back_keep(v):
    return (v, None)

def back_low(kept, grad):
    return (low(grad),)
low.defvjp(low_keep, low_pass)
low_back.defvjp(back_keep, back_low)
NEG_FILL = -1e+30

def both_ways(values):
    return low(low_back(values))

def layer_norm(values, norm_gain, norm_shift):
    center = values - lax.optimization_barrier(jnp.mean(values, -1, keepdims=True))
    variance = lax.optimization_barrier(jnp.mean(center * center, -1, keepdims=True))
    return center * lax.rsqrt(variance + 1e-05) * norm_gain + norm_shift

def allowed_mask(segment, offset, block_size):
    positions = jnp.arange(segment.shape[0])
    query_pos = positions[offset:offset + block_size]
    query_seg = segment[offset:offset + block_size]
    return (positions[None, :] <= query_pos[:, None]) & (segment[None, :] == query_seg[:, None])

def block_forward(pack_tokens, segment, weights):
    ln1_gain, ln1_bias, w_qkv, b_qv, w_out, b_out, ln2_gain, ln2_bias, w_fc, b_fc, w_proj, b_proj = weights
    highest = lax.Precision.HIGHEST
    normed = low(layer_norm(pack_tokens, ln1_gain, ln1_bias))
    packed = jnp.einsum('td,dcn->tcn', normed, w_qkv, precision=highest)
    queries = both_ways(packed[:, 0] + b_qv[0]).reshape(LEN, H, HD)
    key_rows = both_ways(packed[:, 1]).reshape(LEN, H, HD)
    value_rows = both_ways(packed[:, 2] + b_qv[1]).reshape(LEN, H, HD)
    scores = low_back(jnp.einsum('qhe,khe->hqk', queries, key_rows, precision=highest) * HD ** (-0.5))
    allowed = allowed_mask(segment, 0, LEN)
    attn_probs = low(jax.nn.softmax(jnp.where(allowed[None], scores, NEG_FILL), axis=-1))
    mixed_heads = both_ways(jnp.einsum('hqk,khe->qhe', attn_probs, value_rows, precision=highest).reshape(LEN, D))
    residual = pack_tokens + low_back(jnp.dot(mixed_heads, w_out, precision=highest)) + b_out
    normed2 = low(layer_norm(residual, ln2_gain, ln2_bias))
    pre_act = low_back(jnp.dot(normed2, w_fc, precision=highest) + b_fc)
    hidden = low(jax.nn.gelu(pre_act, approximate=True))
    return residual + jnp.dot(hidden, w_proj, precision=highest) + b_proj

def reference(tokens, segment_ids, ln1_gain, ln1_bias, w_qkv, b_qv, w_out, b_out, ln2_gain, ln2_bias, w_fc, b_fc, w_proj, b_proj, cotangent):
    params = jax.tree.map(lambda element: element.astype(jnp.float32), (ln1_gain, ln1_bias, w_qkv, b_qv, w_out, b_out, ln2_gain, ln2_bias, w_fc, b_fc, w_proj, b_proj))
    pack_count = N_DP * PACKS
    tok_packs = tokens.astype(jnp.float32).reshape(pack_count, LEN, D)
    cot_packs = cotangent.astype(jnp.float32).reshape(pack_count, LEN, D)

    def one_pack(totals, inputs):
        pack_tokens, pack_seg, pack_cot = inputs
        outputs, pullback = jax.vjp(lambda tok_in, weights: block_forward(tok_in, pack_seg, weights), pack_tokens, params)
        grad_tok, grad_weights = pullback(pack_cot)
        totals = jax.tree.map(jnp.add, totals, grad_weights)
        return (totals, (outputs.astype(jnp.bfloat16), grad_tok))
    initial = jax.tree.map(jnp.zeros_like, params)
    totals, results = lax.scan(one_pack, initial, (tok_packs, segment_ids, cot_packs))
    out_rows = results[0].reshape(TOKENS, D)
    grad_rows = results[1].reshape(TOKENS, D)
    return (out_rows, grad_rows, totals[0], totals[1], totals[2], totals[3], totals[4], totals[5], totals[6], totals[7], totals[8], totals[9], totals[10], totals[11])
```

```python
import functools

import jax
import jax.numpy as jnp
from jax import lax
from jax.experimental import pallas as pl
from jax.experimental.pallas import tpu as pltpu
from jax.sharding import PartitionSpec as P

HD = 64
LANES = 128
NEG_FILL = -1e30
SCALE = HD ** (-0.5)
F32 = jnp.float32
BF16 = jnp.bfloat16

NT = (((1,), (1,)), ((), ()))
TN = (((0,), (0,)), ((), ()))
NN = (((1,), (0,)), ((), ()))


def mm(a, b, dims=NN):
    return lax.dot_general(a, b, dims, preferred_element_type=F32)


def layer_norm(values, norm_gain, norm_shift):
    center = values - jnp.mean(values, -1, keepdims=True)
    variance = jnp.mean(center * center, -1, keepdims=True)
    return center * lax.rsqrt(variance + 1e-05) * norm_gain + norm_shift


def head_lanes(shape, head):
    lane = lax.broadcasted_iota(jnp.int32, shape, 1)
    return (lane // HD) == head


def only_head(values, head):
    return jnp.where(head_lanes(values.shape, head), values, jnp.zeros_like(values))


def attend_kernel(q_ref, k_ref, v_ref, bias_ref, mixed_ref, lse_ref):
    queries, keys, values = q_ref[...], k_ref[...], v_ref[...]
    mixed = jnp.zeros(queries.shape, F32)
    lse = jnp.zeros(queries.shape, F32)
    for head in range(LANES // HD):
        scores = mm(only_head(queries, head), keys, NT) * SCALE + bias_ref[0]
        top = jnp.max(scores, -1, keepdims=True)
        expo = jnp.exp(scores - top)
        total = jnp.sum(expo, -1, keepdims=True)
        probs = (expo * (1.0 / total)).astype(BF16)
        mine = head_lanes(queries.shape, head)
        mixed = jnp.where(mine, mm(probs, values), mixed)
        lse = jnp.where(mine, top + jnp.log(total), lse)
    mixed_ref[...] = mixed.astype(BF16)
    lse_ref[...] = lse


def attend_back_kernel(q_ref, k_ref, v_ref, bias_ref, g_ref, lse_ref, dq_ref, dk_ref, dv_ref):
    queries, keys, values, grad = q_ref[...], k_ref[...], v_ref[...], g_ref[...]
    dq = jnp.zeros(queries.shape, F32)
    dk = jnp.zeros(keys.shape, F32)
    dv = jnp.zeros(keys.shape, F32)
    for head in range(LANES // HD):
        scores = mm(only_head(queries, head), keys, NT) * SCALE + bias_ref[0]
        probs = jnp.exp(scores - lse_ref[:, head * HD : head * HD + 1])
        grad_probs = mm(only_head(grad, head), values, NT)
        inner = jnp.sum(probs * grad_probs, -1, keepdims=True)
        grad_scores = (probs * (grad_probs - inner)).astype(BF16)
        dq = jnp.where(head_lanes(dq.shape, head), mm(grad_scores, keys), dq)
        dk = jnp.where(head_lanes(dk.shape, head), mm(grad_scores, queries, TN), dk)
        dv = jnp.where(head_lanes(dv.shape, head), mm(probs.astype(BF16), grad, TN), dv)
    dq_ref[...] = (dq * SCALE).astype(BF16)
    dk_ref[...] = (dk * SCALE).astype(BF16)
    dv_ref[...] = dv.astype(BF16)


def attention_call(kernel, bias, arrays, out_types, matmuls, kinds, out_kinds):
    seqs, qlen, klen = bias.shape
    width = arrays[0].shape[1]
    pairs = width // LANES
    spec = {
        "q": pl.BlockSpec((qlen, LANES), lambda s, p: (s, p)),
        "k": pl.BlockSpec((klen, LANES), lambda s, p: (s, p)),
        "b": pl.BlockSpec((1, qlen, klen), lambda s, p: (s, 0, 0)),
    }
    rows = {"q": seqs * qlen, "k": seqs * klen}
    area = seqs * qlen * klen * (width // HD)
    return pl.pallas_call(
        kernel,
        grid=(seqs, pairs),
        in_specs=[spec[kind] for kind in kinds],
        out_specs=[spec[kind] for kind in out_kinds],
        out_shape=[
            jax.ShapeDtypeStruct((rows[kind], width), dtype)
            for kind, dtype in zip(out_kinds, out_types)
        ],
        compiler_params=pltpu.CompilerParams(vmem_limit_bytes=48 * 1024 * 1024),
        cost_estimate=pl.CostEstimate(
            flops=2 * HD * area * matmuls * 4, bytes_accessed=8 * rows["k"] * width, transcendentals=area
        ),
    )(*arrays)


def swap(values, bit, axis="tensor"):
    size = lax.axis_size(axis)
    return lax.ppermute(values, axis, [(i, i ^ bit) for i in range(size)])


def bits_of(count):
    bit, found = 1, []
    while bit < count:
        found.append(bit)
        bit *= 2
    return found


def gather_pieces(own, count):
    pieces = {0: own}
    for bit in reversed(bits_of(count)):
        for j in list(pieces):
            pieces[j ^ bit] = swap(pieces[j], bit)
    return [pieces[j] for j in range(count)]


def reduce_pieces(pieces):
    held = dict(enumerate(pieces))
    for bit in bits_of(len(pieces)):
        held = {
            j: held[j] + swap(held[j ^ bit].astype(BF16), bit).astype(F32)
            for j in held
            if not j & bit
        }
    return held[0]


def reorder(pieces, me, span):
    for bit in bits_of(span):
        odd = (me & bit) != 0
        pieces = [jnp.where(odd, pieces[c ^ bit], pieces[c]) for c in range(len(pieces))]
    return pieces


def split_rows(values, count):
    step = values.shape[0] // count
    return [values[c * step : (c + 1) * step] for c in range(count)]


def on_device(
    tokens,
    segment_ids,
    ln1_gain,
    ln1_bias,
    w_qkv,
    b_qv,
    w_out,
    b_out,
    ln2_gain,
    ln2_bias,
    w_fc,
    b_fc,
    w_proj,
    b_proj,
    cotangent,
):
    count = lax.axis_size("tensor")
    me = lax.axis_index("tensor")
    rows, width = tokens.shape
    seq_len = segment_ids.shape[1]
    local = w_qkv.shape[2]
    span = max(seq_len // rows, 1)
    seqs = max(rows // seq_len, 1)
    qlen = rows // seqs

    own_qkv = w_qkv.transpose(1, 2, 0).reshape(3 * local, width)
    own_bias = jnp.concatenate([b_qv.reshape(-1), b_fc])
    biases = gather_pieces(own_bias, count)
    qkv = reorder(gather_pieces(own_qkv, count), me, span)
    outs = reorder(gather_pieces(w_out, count), me, span)
    fcs = gather_pieces(w_fc, count)
    projs = gather_pieces(w_proj, count)
    bqv = reorder([b[: 2 * local] for b in biases], me, span)
    bfc = [b[2 * local :] for b in biases]
    wq, wk, wv = [
        jnp.concatenate([piece[c * local : (c + 1) * local] for piece in qkv], 0) for c in range(3)
    ]
    bq, bv = [
        jnp.concatenate([piece[c * local : (c + 1) * local] for piece in bqv], 0) for c in range(2)
    ]
    wo = jnp.concatenate(outs, 0)

    first = me * rows // seq_len
    own_segs = lax.dynamic_slice_in_dim(segment_ids, first, seqs, 0)
    starts = [((me ^ o) * rows) % seq_len for o in range(span)]
    parts = [lax.dynamic_slice_in_dim(own_segs, start, qlen, 1) for start in starts]
    places = [start + jnp.arange(qlen) for start in starts]
    key_seg, key_pos = jnp.concatenate(parts, 1), jnp.concatenate(places, 0)
    allowed = (key_pos[None, None, :] <= places[0][None, :, None]) & (
        key_seg[:, None, :] == parts[0][:, :, None]
    )
    mask = jnp.where(allowed, 0.0, NEG_FILL).astype(F32)

    x_full = tokens.astype(F32)
    normed = layer_norm(x_full, ln1_gain, ln1_bias).astype(BF16)
    keys = mm(normed, wk, NT).astype(BF16)
    values = (mm(normed, wv, NT) + bv).astype(BF16)
    keys = jnp.concatenate([keys] + [swap(keys, o) for o in range(1, span)], 0)
    values = jnp.concatenate([values] + [swap(values, o) for o in range(1, span)], 0)
    queries = (mm(normed, wq, NT) + bq).astype(BF16)
    mixed, lse = attention_call(
        attend_kernel, mask, (queries, keys, values, mask), (BF16, F32), 2, "qkkb", "qq"
    )
    residual = x_full + mm(mixed, wo) + b_out
    normed2 = layer_norm(residual, ln2_gain, ln2_bias).astype(BF16)

    gelu = functools.partial(jax.nn.gelu, approximate=True)
    result = residual + b_proj
    d_proj, d_fc, d_bfc = [], [], []
    grad_normed2 = jnp.zeros((rows, width), F32)
    for j in range(count):
        pre_act = mm(normed2, fcs[j]) + bfc[j]
        hidden, gelu_back = jax.vjp(gelu, pre_act)
        hidden = hidden.astype(BF16)
        result = result + mm(hidden, projs[j])
        d_proj.append(mm(hidden, cotangent, TN))
        grad_pre = gelu_back(mm(cotangent, projs[j], NT))[0].astype(BF16)
        d_bfc.append(jnp.sum(grad_pre.astype(F32), 0))
        d_fc.append(mm(normed2, grad_pre, TN))
        grad_normed2 = grad_normed2 + mm(grad_pre, fcs[j], NT)
    output = result.astype(BF16)
    g_proj = lax.psum(reduce_pieces(d_proj).astype(BF16), "dp")
    own_fc, g_proj = lax.optimization_barrier((reduce_pieces(d_fc).astype(BF16), g_proj))
    g_fc = lax.psum(own_fc, "dp")

    cot_full = cotangent.astype(F32)
    _, ln2_back = jax.vjp(layer_norm, residual, ln2_gain, ln2_bias)
    grad_resid_part, d_ln2_gain, d_ln2_bias = ln2_back(grad_normed2)
    grad_resid = cot_full + grad_resid_part
    d_b_proj = jnp.sum(cot_full, 0)
    d_b_out = jnp.sum(grad_resid, 0)
    resid_low = grad_resid.astype(BF16)
    grad_mixed = mm(resid_low, wo, NT).astype(BF16)
    d_out = split_rows(mm(mixed, resid_low, TN), count)
    dq, dk, dv = attention_call(
        attend_back_kernel,
        mask,
        (queries, keys, values, mask, grad_mixed, lse),
        (BF16, BF16, BF16),
        5,
        "qkkbqq",
        "qkk",
    )
    if span > 1:
        dk, dv = [
            sum(
                [swap(grad[o * rows : (o + 1) * rows], o).astype(F32) for o in range(1, span)],
                grad[:rows].astype(F32),
            ).astype(BF16)
            for grad in (dk, dv)
        ]
    d_packed = [split_rows(mm(grad, normed, TN), count) for grad in (dq, dk, dv)]
    d_attn = [
        jnp.concatenate([d_packed[0][c], d_packed[1][c], d_packed[2][c], d_out[c]], 0)
        for c in range(count)
    ]
    own_attn = reduce_pieces(reorder(d_attn, me, span)).astype(BF16)
    own_attn, g_fc = lax.optimization_barrier((own_attn, g_fc))
    g_attn = lax.psum(own_attn, "dp")
    d_bq = split_rows(jnp.sum(dq.astype(F32), 0), count)
    d_bv = split_rows(jnp.sum(dv.astype(F32), 0), count)
    d_bqv = reorder([jnp.concatenate([d_bq[c], d_bv[c]]) for c in range(count)], me, span)

    grad_normed = mm(dq, wq) + mm(dk, wk) + mm(dv, wv)
    _, ln1_back = jax.vjp(layer_norm, x_full, ln1_gain, ln1_bias)
    grad_tok_part, d_ln1_gain, d_ln1_bias = ln1_back(grad_normed)
    d_tokens = grad_resid + grad_tok_part

    shared = jnp.stack([d_ln1_gain, d_ln1_bias, d_b_out, d_ln2_gain, d_ln2_bias, d_b_proj])
    held = {j: jnp.concatenate([d_bqv[j], d_bfc[j]]) for j in range(count)}
    for bit in bits_of(count):
        send = jnp.concatenate([held[j] for j in held if j & bit] + [shared.reshape(-1)])
        got = swap(send, bit)
        keep = [j for j in held if not j & bit]
        size = held[0].shape[0]
        order = [j ^ bit for j in held if j & bit]
        held = {
            j: held[j] + got[order.index(j) * size : (order.index(j) + 1) * size] for j in keep
        }
        shared = shared + got[len(order) * size :].reshape(shared.shape)
    small = jnp.concatenate([held[0], shared.reshape(-1)])
    for bit in bits_of(lax.axis_size("dp")):
        small = small + swap(small, bit, "dp")
    d_b_qv = small[: 2 * local].reshape(2, local)
    d_b_fc = small[2 * local : held[0].shape[0]]
    shared = small[held[0].shape[0] :].reshape(shared.shape)

    d_w_qkv = g_attn[: 3 * local].astype(F32).reshape(3, local, width).transpose(2, 0, 1)
    d_w_out = g_attn[3 * local :].astype(F32)
    return (
        output,
        d_tokens,
        shared[0],
        shared[1],
        d_w_qkv,
        d_b_qv,
        d_w_out,
        shared[2],
        shared[3],
        shared[4],
        g_fc.astype(F32),
        d_b_fc,
        g_proj.astype(F32),
        shared[5],
    )


def solution(mesh):
    return jax.shard_map(
        on_device,
        mesh=mesh,
        in_specs=(
            P(("dp", "tensor"), None),
            P("dp", None),
            P(),
            P(),
            P(None, None, "tensor"),
            P(None, "tensor"),
            P("tensor", None),
            P(),
            P(),
            P(),
            P(None, "tensor"),
            P("tensor"),
            P("tensor", None),
            P(),
            P(("dp", "tensor"), None),
        ),
        out_specs=(
            P(("dp", "tensor"), None),
            P(("dp", "tensor"), None),
            P(),
            P(),
            P(None, None, "tensor"),
            P(None, "tensor"),
            P("tensor", None),
            P(),
            P(),
            P(),
            P(None, "tensor"),
            P("tensor"),
            P("tensor", None),
            P(),
        ),
        check_vma=False,
    )
```

```python
import functools

import jax
import jax.numpy as jnp
from jax import lax
from jax.experimental import pallas as pl
from jax.experimental.pallas import tpu as pltpu
from jax.sharding import PartitionSpec as P

HD = 64
LANES = 128
NEG_FILL = -1e30
SCALE = HD ** (-0.5)
F32 = jnp.float32
BF16 = jnp.bfloat16

NT = (((1,), (1,)), ((), ()))
TN = (((0,), (0,)), ((), ()))
NN = (((1,), (0,)), ((), ()))


def mm(a, b, dims=NN):
    return lax.dot_general(a, b, dims, preferred_element_type=F32)


def layer_norm(values, norm_gain, norm_shift):
    center = values - jnp.mean(values, -1, keepdims=True)
    variance = jnp.mean(center * center, -1, keepdims=True)
    return center * lax.rsqrt(variance + 1e-05) * norm_gain + norm_shift


def head_lanes(shape, head):
    lane = lax.broadcasted_iota(jnp.int32, shape, 1)
    return (lane // HD) == head


def only_head(values, head):
    return jnp.where(head_lanes(values.shape, head), values, jnp.zeros_like(values))


def attend_kernel(q_ref, k_ref, v_ref, bias_ref, mixed_ref, lse_ref):
    queries, keys, values = q_ref[...], k_ref[...], v_ref[...]
    mixed = jnp.zeros(queries.shape, F32)
    lse = jnp.zeros(queries.shape, F32)
    for head in range(LANES // HD):
        scores = mm(only_head(queries, head), keys, NT) * SCALE + bias_ref[0]
        top = jnp.max(scores, -1, keepdims=True)
        expo = jnp.exp(scores - top)
        total = jnp.sum(expo, -1, keepdims=True)
        probs = (expo * (1.0 / total)).astype(BF16)
        mine = head_lanes(queries.shape, head)
        mixed = jnp.where(mine, mm(probs, values), mixed)
        lse = jnp.where(mine, top + jnp.log(total), lse)
    mixed_ref[...] = mixed.astype(BF16)
    lse_ref[...] = lse


def attend_back_kernel(q_ref, k_ref, v_ref, bias_ref, g_ref, lse_ref, dq_ref, dk_ref, dv_ref):
    queries, keys, values, grad = q_ref[...], k_ref[...], v_ref[...], g_ref[...]
    dq = jnp.zeros(queries.shape, F32)
    dk = jnp.zeros(keys.shape, F32)
    dv = jnp.zeros(keys.shape, F32)
    for head in range(LANES // HD):
        scores = mm(only_head(queries, head), keys, NT) * SCALE + bias_ref[0]
        probs = jnp.exp(scores - lse_ref[:, head * HD : head * HD + 1])
        grad_probs = mm(only_head(grad, head), values, NT)
        inner = jnp.sum(probs * grad_probs, -1, keepdims=True)
        grad_scores = (probs * (grad_probs - inner)).astype(BF16)
        dq = jnp.where(head_lanes(dq.shape, head), mm(grad_scores, keys), dq)
        dk = jnp.where(head_lanes(dk.shape, head), mm(grad_scores, queries, TN), dk)
        dv = jnp.where(head_lanes(dv.shape, head), mm(probs.astype(BF16), grad, TN), dv)
    dq_ref[...] = (dq * SCALE).astype(BF16)
    dk_ref[...] = (dk * SCALE).astype(BF16)
    dv_ref[...] = dv.astype(BF16)


def attention_call(kernel, bias, arrays, out_types, matmuls, kinds, out_kinds):
    seqs, qlen, klen = bias.shape
    width = arrays[0].shape[1]
    pairs = width // LANES
    spec = {
        "q": pl.BlockSpec((qlen, LANES), lambda s, p: (s, p)),
        "k": pl.BlockSpec((klen, LANES), lambda s, p: (s, p)),
        "b": pl.BlockSpec((1, qlen, klen), lambda s, p: (s, 0, 0)),
    }
    rows = {"q": seqs * qlen, "k": seqs * klen}
    area = seqs * qlen * klen * (width // HD)
    return pl.pallas_call(
        kernel,
        grid=(seqs, pairs),
        in_specs=[spec[kind] for kind in kinds],
        out_specs=[spec[kind] for kind in out_kinds],
        out_shape=[
            jax.ShapeDtypeStruct((rows[kind], width), dtype)
            for kind, dtype in zip(out_kinds, out_types)
        ],
        compiler_params=pltpu.CompilerParams(vmem_limit_bytes=48 * 1024 * 1024),
        cost_estimate=pl.CostEstimate(
            flops=2 * HD * area * matmuls * 4, bytes_accessed=8 * rows["k"] * width, transcendentals=area
        ),
    )(*arrays)


def swap(values, bit, axis="tensor"):
    size = lax.axis_size(axis)
    return lax.ppermute(values, axis, [(i, i ^ bit) for i in range(size)])


def bits_of(count):
    bit, found = 1, []
    while bit < count:
        found.append(bit)
        bit *= 2
    return found


def gather_pieces(own, count):
    pieces = {0: own}
    for bit in reversed(bits_of(count)):
        for j in list(pieces):
            pieces[j ^ bit] = swap(pieces[j], bit)
    return [pieces[j] for j in range(count)]


def reduce_start(pieces):
    held = dict(enumerate(pieces))
    bits = bits_of(len(pieces))
    for bit in bits[:-1]:
        held = {
            j: held[j] + swap(held[j ^ bit].astype(BF16), bit).astype(F32)
            for j in held
            if not j & bit
        }
    return held[0], held[bits[-1]].astype(BF16)


def reduce_finish(own, send, count):
    return own + swap(send, bits_of(count)[-1]).astype(F32)


def all_sum(values, bits):
    me = lax.axis_index("dp")
    for bit in bits:
        upper = (me & bit) != 0
        half = values.shape[0] // 2
        low, high = values[:half], values[half:]
        send = jnp.where(upper, low, high).astype(BF16)
        values = jnp.where(upper, high, low) + swap(send, bit, "dp").astype(F32)
    values = values.astype(BF16)
    for bit in reversed(bits):
        upper = (me & bit) != 0
        got = swap(values, bit, "dp")
        values = jnp.concatenate(
            [jnp.where(upper, got, values), jnp.where(upper, values, got)], 0
        )
    return values


def reorder(pieces, me, span):
    for bit in bits_of(span):
        odd = (me & bit) != 0
        pieces = [jnp.where(odd, pieces[c ^ bit], pieces[c]) for c in range(len(pieces))]
    return pieces


def split_rows(values, count):
    step = values.shape[0] // count
    return [values[c * step : (c + 1) * step] for c in range(count)]


def on_device(
    tokens,
    segment_ids,
    ln1_gain,
    ln1_bias,
    w_qkv,
    b_qv,
    w_out,
    b_out,
    ln2_gain,
    ln2_bias,
    w_fc,
    b_fc,
    w_proj,
    b_proj,
    cotangent,
):
    count = lax.axis_size("tensor")
    me = lax.axis_index("tensor")
    rows, width = tokens.shape
    seq_len = segment_ids.shape[1]
    local = w_qkv.shape[2]
    span = max(seq_len // rows, 1)
    seqs = max(rows // seq_len, 1)
    qlen = rows // seqs

    own_qkv = w_qkv.transpose(1, 2, 0).reshape(3 * local, width)
    own_bias = jnp.concatenate([b_qv.reshape(-1), b_fc])
    biases = gather_pieces(own_bias, count)
    qkv = gather_pieces(own_qkv, count)
    far = bits_of(count)[-1]
    qkv[far], w_out = lax.optimization_barrier((qkv[far], w_out))
    qkv = reorder(qkv, me, span)
    outs = gather_pieces(w_out, count)
    outs[far], w_fc = lax.optimization_barrier((outs[far], w_fc))
    outs = reorder(outs, me, span)
    fcs = gather_pieces(w_fc, count)
    fcs[far], w_proj = lax.optimization_barrier((fcs[far], w_proj))
    projs = gather_pieces(w_proj, count)
    bqv = reorder([b[: 2 * local] for b in biases], me, span)
    bfc = [b[2 * local :] for b in biases]
    wq, wk, wv = [
        jnp.concatenate([piece[c * local : (c + 1) * local] for piece in qkv], 0) for c in range(3)
    ]
    bq, bv = [
        jnp.concatenate([piece[c * local : (c + 1) * local] for piece in bqv], 0) for c in range(2)
    ]
    wo = jnp.concatenate(outs, 0)

    first = me * rows // seq_len
    own_segs = lax.dynamic_slice_in_dim(segment_ids, first, seqs, 0)
    starts = [((me ^ o) * rows) % seq_len for o in range(span)]
    parts = [lax.dynamic_slice_in_dim(own_segs, start, qlen, 1) for start in starts]
    places = [start + jnp.arange(qlen) for start in starts]
    key_seg, key_pos = jnp.concatenate(parts, 1), jnp.concatenate(places, 0)
    allowed = (key_pos[None, None, :] <= places[0][None, :, None]) & (
        key_seg[:, None, :] == parts[0][:, :, None]
    )
    mask = jnp.where(allowed, 0.0, NEG_FILL).astype(F32)

    x_full = tokens.astype(F32)
    normed = layer_norm(x_full, ln1_gain, ln1_bias).astype(BF16)
    keys = mm(normed, wk, NT).astype(BF16)
    values = (mm(normed, wv, NT) + bv).astype(BF16)
    keys = jnp.concatenate([keys] + [swap(keys, o) for o in range(1, span)], 0)
    values = jnp.concatenate([values] + [swap(values, o) for o in range(1, span)], 0)
    queries = (mm(normed, wq, NT) + bq).astype(BF16)
    mixed, lse = attention_call(
        attend_kernel, mask, (queries, keys, values, mask), (BF16, F32), 2, "qkkb", "qq"
    )
    residual = x_full + mm(mixed, wo) + b_out
    normed2 = layer_norm(residual, ln2_gain, ln2_bias).astype(BF16)

    gelu = functools.partial(jax.nn.gelu, approximate=True)
    result = residual + b_proj
    d_proj, d_fc, d_bfc = [], [], []
    grad_normed2 = jnp.zeros((rows, width), F32)
    for j in range(count):
        pre_act = mm(normed2, fcs[j]) + bfc[j]
        hidden, gelu_back = jax.vjp(gelu, pre_act)
        hidden = hidden.astype(BF16)
        result = result + mm(hidden, projs[j])
        d_proj.append(mm(hidden, cotangent, TN))
        grad_pre = gelu_back(mm(cotangent, projs[j], NT))[0].astype(BF16)
        d_bfc.append(jnp.sum(grad_pre.astype(F32), 0))
        d_fc.append(mm(normed2, grad_pre, TN))
        grad_normed2 = grad_normed2 + mm(grad_pre, fcs[j], NT)
    output = result.astype(BF16)
    own_proj, send_proj = reduce_start(d_proj)
    own_fc, send_fc = reduce_start(d_fc)

    cot_full = cotangent.astype(F32)
    _, ln2_back = jax.vjp(layer_norm, residual, ln2_gain, ln2_bias)
    grad_resid_part, d_ln2_gain, d_ln2_bias = ln2_back(grad_normed2)
    grad_resid = cot_full + grad_resid_part
    d_b_proj = jnp.sum(cot_full, 0)
    d_b_out = jnp.sum(grad_resid, 0)
    resid_low = grad_resid.astype(BF16)
    grad_mixed = mm(resid_low, wo, NT).astype(BF16)
    grad_mixed, send_proj, send_fc = lax.optimization_barrier((grad_mixed, send_proj, send_fc))
    bits = bits_of(lax.axis_size("dp"))
    turned = bits[1:] + bits[:1]
    own_proj = reduce_finish(own_proj, send_proj, count)
    own_fc = reduce_finish(own_fc, send_fc, count)
    d_out = split_rows(mm(mixed, resid_low, TN), count)
    dq, dk, dv = attention_call(
        attend_back_kernel,
        mask,
        (queries, keys, values, mask, grad_mixed, lse),
        (BF16, BF16, BF16),
        5,
        "qkkbqq",
        "qkk",
    )
    if span > 1:
        dk, dv = [
            sum(
                [swap(grad[o * rows : (o + 1) * rows], o).astype(F32) for o in range(1, span)],
                grad[:rows].astype(F32),
            ).astype(BF16)
            for grad in (dk, dv)
        ]
    d_packed = [split_rows(mm(grad, normed, TN), count) for grad in (dq, dk, dv)]
    d_attn = [
        jnp.concatenate([d_packed[0][c], d_packed[1][c], d_packed[2][c], d_out[c]], 0)
        for c in range(count)
    ]
    own_attn = reduce_finish(*reduce_start(reorder(d_attn, me, span)), count)
    g_proj = all_sum(own_proj, bits)
    g_fc = all_sum(own_fc, turned)
    g_attn = all_sum(own_attn, bits)
    d_bq = split_rows(jnp.sum(dq.astype(F32), 0), count)
    d_bv = split_rows(jnp.sum(dv.astype(F32), 0), count)
    d_bqv = reorder([jnp.concatenate([d_bq[c], d_bv[c]]) for c in range(count)], me, span)

    grad_normed = mm(dq, wq) + mm(dk, wk) + mm(dv, wv)
    _, ln1_back = jax.vjp(layer_norm, x_full, ln1_gain, ln1_bias)
    grad_tok_part, d_ln1_gain, d_ln1_bias = ln1_back(grad_normed)
    d_tokens = grad_resid + grad_tok_part

    shared = jnp.stack([d_ln1_gain, d_ln1_bias, d_b_out, d_ln2_gain, d_ln2_bias, d_b_proj])
    held = {j: jnp.concatenate([d_bqv[j], d_bfc[j]]) for j in range(count)}
    for bit in bits_of(count):
        send = jnp.concatenate([held[j] for j in held if j & bit] + [shared.reshape(-1)])
        got = swap(send, bit)
        keep = [j for j in held if not j & bit]
        size = held[0].shape[0]
        order = [j ^ bit for j in held if j & bit]
        held = {
            j: held[j] + got[order.index(j) * size : (order.index(j) + 1) * size] for j in keep
        }
        shared = shared + got[len(order) * size :].reshape(shared.shape)
    small = jnp.concatenate([held[0], shared.reshape(-1)])
    for bit in bits_of(lax.axis_size("dp")):
        small = small + swap(small, bit, "dp")
    d_b_qv = small[: 2 * local].reshape(2, local)
    d_b_fc = small[2 * local : held[0].shape[0]]
    shared = small[held[0].shape[0] :].reshape(shared.shape)

    d_w_qkv = g_attn[: 3 * local].astype(F32).reshape(3, local, width).transpose(2, 0, 1)
    d_w_out = g_attn[3 * local :].astype(F32)
    return (
        output,
        d_tokens,
        shared[0],
        shared[1],
        d_w_qkv,
        d_b_qv,
        d_w_out,
        shared[2],
        shared[3],
        shared[4],
        g_fc.astype(F32),
        d_b_fc,
        g_proj.astype(F32),
        shared[5],
    )


def solution(mesh):
    return jax.shard_map(
        on_device,
        mesh=mesh,
        in_specs=(
            P(("dp", "tensor"), None),
            P("dp", None),
            P(),
            P(),
            P(None, None, "tensor"),
            P(None, "tensor"),
            P("tensor", None),
            P(),
            P(),
            P(),
            P(None, "tensor"),
            P("tensor"),
            P("tensor", None),
            P(),
            P(("dp", "tensor"), None),
        ),
        out_specs=(
            P(("dp", "tensor"), None),
            P(("dp", "tensor"), None),
            P(),
            P(),
            P(None, None, "tensor"),
            P(None, "tensor"),
            P("tensor", None),
            P(),
            P(),
            P(),
            P(None, "tensor"),
            P("tensor"),
            P("tensor", None),
            P(),
        ),
        check_vma=False,
    )
```

```python
import functools

import jax
import jax.numpy as jnp
from jax import lax
from jax.experimental import pallas as pl
from jax.experimental.pallas import tpu as pltpu
from jax.sharding import PartitionSpec as P

HD = 64
LANES = 128
NEG_FILL = -1e30
SCALE = HD ** (-0.5)
F32 = jnp.float32
BF16 = jnp.bfloat16

NT = (((1,), (1,)), ((), ()))
TN = (((0,), (0,)), ((), ()))
NN = (((1,), (0,)), ((), ()))


def mm(a, b, dims=NN):
    return lax.dot_general(a, b, dims, preferred_element_type=F32)


def layer_norm(values, norm_gain, norm_shift):
    center = values - jnp.mean(values, -1, keepdims=True)
    variance = jnp.mean(center * center, -1, keepdims=True)
    return center * lax.rsqrt(variance + 1e-05) * norm_gain + norm_shift


def head_lanes(shape, head):
    lane = lax.broadcasted_iota(jnp.int32, shape, 1)
    return (lane // HD) == head


def only_head(values, head):
    return jnp.where(head_lanes(values.shape, head), values, jnp.zeros_like(values))


def attend_kernel(q_ref, k_ref, v_ref, bias_ref, mixed_ref, lse_ref):
    queries, keys, values = q_ref[...], k_ref[...], v_ref[...]
    mixed = jnp.zeros(queries.shape, F32)
    lse = jnp.zeros(queries.shape, F32)
    for head in range(LANES // HD):
        scores = mm(only_head(queries, head), keys, NT) * SCALE + bias_ref[0]
        top = jnp.max(scores, -1, keepdims=True)
        expo = jnp.exp(scores - top)
        total = jnp.sum(expo, -1, keepdims=True)
        probs = (expo * (1.0 / total)).astype(BF16)
        mine = head_lanes(queries.shape, head)
        mixed = jnp.where(mine, mm(probs, values), mixed)
        lse = jnp.where(mine, top + jnp.log(total), lse)
    mixed_ref[...] = mixed.astype(BF16)
    lse_ref[...] = lse


def attend_back_kernel(q_ref, k_ref, v_ref, bias_ref, g_ref, lse_ref, dq_ref, dk_ref, dv_ref):
    queries, keys, values, grad = q_ref[...], k_ref[...], v_ref[...], g_ref[...]
    dq = jnp.zeros(queries.shape, F32)
    dk = jnp.zeros(keys.shape, F32)
    dv = jnp.zeros(keys.shape, F32)
    for head in range(LANES // HD):
        scores = mm(only_head(queries, head), keys, NT) * SCALE + bias_ref[0]
        probs = jnp.exp(scores - lse_ref[:, head * HD : head * HD + 1])
        grad_probs = mm(only_head(grad, head), values, NT)
        inner = jnp.sum(probs * grad_probs, -1, keepdims=True)
        grad_scores = (probs * (grad_probs - inner)).astype(BF16)
        dq = jnp.where(head_lanes(dq.shape, head), mm(grad_scores, keys), dq)
        dk = jnp.where(head_lanes(dk.shape, head), mm(grad_scores, queries, TN), dk)
        dv = jnp.where(head_lanes(dv.shape, head), mm(probs.astype(BF16), grad, TN), dv)
    dq_ref[...] = (dq * SCALE).astype(BF16)
    dk_ref[...] = (dk * SCALE).astype(BF16)
    dv_ref[...] = dv.astype(BF16)


def attention_call(kernel, bias, arrays, out_types, matmuls, kinds, out_kinds):
    seqs, qlen, klen = bias.shape
    width = arrays[0].shape[1]
    pairs = width // LANES
    spec = {
        "q": pl.BlockSpec((qlen, LANES), lambda s, p: (s, p)),
        "k": pl.BlockSpec((klen, LANES), lambda s, p: (s, p)),
        "b": pl.BlockSpec((1, qlen, klen), lambda s, p: (s, 0, 0)),
    }
    rows = {"q": seqs * qlen, "k": seqs * klen}
    area = seqs * qlen * klen * (width // HD)
    return pl.pallas_call(
        kernel,
        grid=(seqs, pairs),
        in_specs=[spec[kind] for kind in kinds],
        out_specs=[spec[kind] for kind in out_kinds],
        out_shape=[
            jax.ShapeDtypeStruct((rows[kind], width), dtype)
            for kind, dtype in zip(out_kinds, out_types)
        ],
        compiler_params=pltpu.CompilerParams(vmem_limit_bytes=48 * 1024 * 1024),
        cost_estimate=pl.CostEstimate(
            flops=2 * HD * area * matmuls * 4, bytes_accessed=8 * rows["k"] * width, transcendentals=area
        ),
    )(*arrays)


def swap(values, bit, axis="tensor"):
    size = lax.axis_size(axis)
    return lax.ppermute(values, axis, [(i, i ^ bit) for i in range(size)])


def bits_of(count):
    bit, found = 1, []
    while bit < count:
        found.append(bit)
        bit *= 2
    return found


def gather_pieces(own, count):
    pieces = {0: own}
    for bit in reversed(bits_of(count)):
        for j in list(pieces):
            pieces[j ^ bit] = swap(pieces[j], bit)
    return [pieces[j] for j in range(count)]


def reduce_start(pieces):
    held = dict(enumerate(pieces))
    bits = bits_of(len(pieces))
    for bit in bits[:-1]:
        held = {
            j: held[j] + swap(held[j ^ bit].astype(BF16), bit).astype(F32)
            for j in held
            if not j & bit
        }
    return held[0], held[bits[-1]].astype(BF16)


def reduce_finish(own, send, count):
    return own + swap(send, bits_of(count)[-1]).astype(F32)


def all_sum(values, bits):
    me = lax.axis_index("dp")
    for bit in bits:
        upper = (me & bit) != 0
        half = values.shape[0] // 2
        low, high = values[:half], values[half:]
        send = jnp.where(upper, low, high).astype(BF16)
        values = jnp.where(upper, high, low) + swap(send, bit, "dp").astype(F32)
    values = values.astype(BF16)
    for bit in reversed(bits):
        upper = (me & bit) != 0
        got = swap(values, bit, "dp")
        values = jnp.concatenate(
            [jnp.where(upper, got, values), jnp.where(upper, values, got)], 0
        )
    return values


def reorder(pieces, me, span):
    for bit in bits_of(span):
        odd = (me & bit) != 0
        pieces = [jnp.where(odd, pieces[c ^ bit], pieces[c]) for c in range(len(pieces))]
    return pieces


def split_rows(values, count):
    step = values.shape[0] // count
    return [values[c * step : (c + 1) * step] for c in range(count)]


def on_device(
    tokens,
    segment_ids,
    ln1_gain,
    ln1_bias,
    w_qkv,
    b_qv,
    w_out,
    b_out,
    ln2_gain,
    ln2_bias,
    w_fc,
    b_fc,
    w_proj,
    b_proj,
    cotangent,
):
    count = lax.axis_size("tensor")
    me = lax.axis_index("tensor")
    rows, width = tokens.shape
    seq_len = segment_ids.shape[1]
    local = w_qkv.shape[2]
    span = max(seq_len // rows, 1)
    seqs = max(rows // seq_len, 1)
    qlen = rows // seqs

    own_qkv = w_qkv.transpose(1, 2, 0).reshape(3 * local, width)
    own_bias = jnp.concatenate([b_qv.reshape(-1), b_fc])
    biases = gather_pieces(own_bias, count)
    qkv = gather_pieces(own_qkv, count)
    far = bits_of(count)[-1]
    qkv[far], w_out = lax.optimization_barrier((qkv[far], w_out))
    qkv = reorder(qkv, me, span)
    outs = gather_pieces(w_out, count)
    outs[far], w_fc = lax.optimization_barrier((outs[far], w_fc))
    outs = reorder(outs, me, span)
    fcs = gather_pieces(w_fc, count)
    fcs[far], w_proj = lax.optimization_barrier((fcs[far], w_proj))
    projs = gather_pieces(w_proj, count)
    bqv = reorder([b[: 2 * local] for b in biases], me, span)
    bfc = [b[2 * local :] for b in biases]
    wq, wk, wv = [
        jnp.concatenate([piece[c * local : (c + 1) * local] for piece in qkv], 0) for c in range(3)
    ]
    bq, bv = [
        jnp.concatenate([piece[c * local : (c + 1) * local] for piece in bqv], 0) for c in range(2)
    ]
    wo = jnp.concatenate(outs, 0)

    first = me * rows // seq_len
    own_segs = lax.dynamic_slice_in_dim(segment_ids, first, seqs, 0)
    starts = [((me ^ o) * rows) % seq_len for o in range(span)]
    parts = [lax.dynamic_slice_in_dim(own_segs, start, qlen, 1) for start in starts]
    places = [start + jnp.arange(qlen) for start in starts]
    key_seg, key_pos = jnp.concatenate(parts, 1), jnp.concatenate(places, 0)
    allowed = (key_pos[None, None, :] <= places[0][None, :, None]) & (
        key_seg[:, None, :] == parts[0][:, :, None]
    )
    mask = jnp.where(allowed, 0.0, NEG_FILL).astype(F32)

    x_full = tokens.astype(F32)
    normed = layer_norm(x_full, ln1_gain, ln1_bias).astype(BF16)
    keys = mm(normed, wk, NT).astype(BF16)
    values = (mm(normed, wv, NT) + bv).astype(BF16)
    keys = jnp.concatenate([keys] + [swap(keys, o) for o in range(1, span)], 0)
    values = jnp.concatenate([values] + [swap(values, o) for o in range(1, span)], 0)
    queries = (mm(normed, wq, NT) + bq).astype(BF16)
    mixed, lse = attention_call(
        attend_kernel, mask, (queries, keys, values, mask), (BF16, F32), 2, "qkkb", "qq"
    )
    residual = x_full + mm(mixed, wo) + b_out
    normed2 = layer_norm(residual, ln2_gain, ln2_bias).astype(BF16)

    gelu = functools.partial(jax.nn.gelu, approximate=True)
    result = residual + b_proj
    d_proj, d_fc, d_bfc = [], [], []
    grad_normed2 = jnp.zeros((rows, width), F32)
    for j in range(count):
        pre_act = mm(normed2, fcs[j]) + bfc[j]
        hidden, gelu_back = jax.vjp(gelu, pre_act)
        hidden = hidden.astype(BF16)
        result = result + mm(hidden, projs[j])
        d_proj.append(mm(hidden, cotangent, TN))
        grad_pre = gelu_back(mm(cotangent, projs[j], NT))[0].astype(BF16)
        d_bfc.append(jnp.sum(grad_pre.astype(F32), 0))
        d_fc.append(mm(normed2, grad_pre, TN))
        grad_normed2 = grad_normed2 + mm(grad_pre, fcs[j], NT)
    output = result.astype(BF16)
    own_proj, send_proj = reduce_start(d_proj)
    own_fc, send_fc = reduce_start(d_fc)

    cot_full = cotangent.astype(F32)
    _, ln2_back = jax.vjp(layer_norm, residual, ln2_gain, ln2_bias)
    grad_resid_part, d_ln2_gain, d_ln2_bias = ln2_back(grad_normed2)
    grad_resid = cot_full + grad_resid_part
    d_b_proj = jnp.sum(cot_full, 0)
    d_b_out = jnp.sum(grad_resid, 0)
    resid_low = grad_resid.astype(BF16)
    grad_mixed = mm(resid_low, wo, NT).astype(BF16)
    grad_mixed, send_proj, send_fc = lax.optimization_barrier((grad_mixed, send_proj, send_fc))
    bits = bits_of(lax.axis_size("dp"))
    turned = bits[1:] + bits[:1]
    got_proj = swap(send_proj, far)
    own_fc = reduce_finish(own_fc, send_fc, count)
    d_out = split_rows(mm(mixed, resid_low, TN), count)
    dq, dk, dv = attention_call(
        attend_back_kernel,
        mask,
        (queries, keys, values, mask, grad_mixed, lse),
        (BF16, BF16, BF16),
        5,
        "qkkbqq",
        "qkk",
    )
    dq, dk, dv, got_proj = lax.optimization_barrier((dq, dk, dv, got_proj))
    own_proj = own_proj + got_proj.astype(F32)
    if span > 1:
        dk, dv = [
            sum(
                [swap(grad[o * rows : (o + 1) * rows], o).astype(F32) for o in range(1, span)],
                grad[:rows].astype(F32),
            ).astype(BF16)
            for grad in (dk, dv)
        ]
    d_packed = [split_rows(mm(grad, normed, TN), count) for grad in (dq, dk, dv)]
    d_attn = [
        jnp.concatenate([d_packed[0][c], d_packed[1][c], d_packed[2][c], d_out[c]], 0)
        for c in range(count)
    ]
    own_attn = reduce_finish(*reduce_start(reorder(d_attn, me, span)), count)
    g_proj = all_sum(own_proj, bits)
    g_fc = all_sum(own_fc, turned)
    d_bq = split_rows(jnp.sum(dq.astype(F32), 0), count)
    d_bv = split_rows(jnp.sum(dv.astype(F32), 0), count)
    d_bqv = reorder([jnp.concatenate([d_bq[c], d_bv[c]]) for c in range(count)], me, span)

    grad_normed = mm(dq, wq) + mm(dk, wk) + mm(dv, wv)
    _, ln1_back = jax.vjp(layer_norm, x_full, ln1_gain, ln1_bias)
    grad_tok_part, d_ln1_gain, d_ln1_bias = ln1_back(grad_normed)
    d_tokens = grad_resid + grad_tok_part

    shared = jnp.stack([d_ln1_gain, d_ln1_bias, d_b_out, d_ln2_gain, d_ln2_bias, d_b_proj])
    shared, own_attn = lax.optimization_barrier((shared, own_attn))
    g_attn = all_sum(own_attn, bits)
    held = {j: jnp.concatenate([d_bqv[j], d_bfc[j]]) for j in range(count)}
    for bit in bits_of(count):
        send = jnp.concatenate([held[j] for j in held if j & bit] + [shared.reshape(-1)])
        got = swap(send, bit)
        keep = [j for j in held if not j & bit]
        size = held[0].shape[0]
        order = [j ^ bit for j in held if j & bit]
        held = {
            j: held[j] + got[order.index(j) * size : (order.index(j) + 1) * size] for j in keep
        }
        shared = shared + got[len(order) * size :].reshape(shared.shape)
    small = jnp.concatenate([held[0], shared.reshape(-1)])
    for bit in bits_of(lax.axis_size("dp")):
        small = small + swap(small, bit, "dp")
    d_b_qv = small[: 2 * local].reshape(2, local)
    d_b_fc = small[2 * local : held[0].shape[0]]
    shared = small[held[0].shape[0] :].reshape(shared.shape)

    d_w_qkv = g_attn[: 3 * local].astype(F32).reshape(3, local, width).transpose(2, 0, 1)
    d_w_out = g_attn[3 * local :].astype(F32)
    return (
        output,
        d_tokens,
        shared[0],
        shared[1],
        d_w_qkv,
        d_b_qv,
        d_w_out,
        shared[2],
        shared[3],
        shared[4],
        g_fc.astype(F32),
        d_b_fc,
        g_proj.astype(F32),
        shared[5],
    )


def solution(mesh):
    return jax.shard_map(
        on_device,
        mesh=mesh,
        in_specs=(
            P(("dp", "tensor"), None),
            P("dp", None),
            P(),
            P(),
            P(None, None, "tensor"),
            P(None, "tensor"),
            P("tensor", None),
            P(),
            P(),
            P(),
            P(None, "tensor"),
            P("tensor"),
            P("tensor", None),
            P(),
            P(("dp", "tensor"), None),
        ),
        out_specs=(
            P(("dp", "tensor"), None),
            P(("dp", "tensor"), None),
            P(),
            P(),
            P(None, None, "tensor"),
            P(None, "tensor"),
            P("tensor", None),
            P(),
            P(),
            P(),
            P(None, "tensor"),
            P("tensor"),
            P("tensor", None),
            P(),
        ),
        check_vma=False,
    )
```
